32 devices in a mesh: fsdp: 16 (over z, x, core), seq: 2 (over y).
Axes of the slice: x: 2, y: 2, z: 4, core: 2. Of those that a mesh axis runs over, the one named last changes fastest.
Arguments:
- latents: float32 [32, 128, 768], P('fsdp', 'seq'), may hold values from -6 to 6
- cond_pick: int32 [32], P('fsdp'), may hold values from 0 to 999
- cond_table: float32 [1000, 768], replicated, may hold values from -6 to 6
- w_ada: bfloat16 [2, 768, 4608], P(None, None, ('fsdp', 'seq')), may hold values from -0.21875 to 0.21875
- b_ada: bfloat16 [2, 4608], P(None, ('fsdp', 'seq')), may hold values from -3 to 3
- w_qkv: bfloat16 [2, 768, 2304], P(None, None, ('fsdp', 'seq')), may hold values from -0.21875 to 0.21875
- w_out: bfloat16 [2, 768, 768], P(None, None, ('fsdp', 'seq')), may hold values from -1.5 to 1.5
- w_up: bfloat16 [2, 768, 3072], P(None, None, ('fsdp', 'seq')), may hold values from -0.21875 to 0.21875
- w_down: bfloat16 [2, 3072, 768], P(None, ('fsdp', 'seq')), may hold values from -0.109375 to 0.109375
- cotangent: float32 [32, 128, 768], P('fsdp', 'seq'), may hold values from -6 to 6
Outputs:
- output: float32 [32, 128, 768], P('fsdp', 'seq')
- grad_latents: float32 [32, 128, 768], P('fsdp', 'seq')
- grad_table: float32 [1000, 768], P(None, ('fsdp', 'seq'))
- grad_w_ada: float32 [2, 768, 4608], P(None, None, ('fsdp', 'seq'))
- grad_b_ada: float32 [2, 4608], P(None, ('fsdp', 'seq'))
- grad_w_qkv: float32 [2, 768, 2304], P(None, None, ('fsdp', 'seq'))
- grad_w_out: float32 [2, 768, 768], P(None, None, ('fsdp', 'seq'))
- grad_w_up: float32 [2, 768, 3072], P(None, None, ('fsdp', 'seq'))
- grad_w_down: float32 [2, 3072, 768], P(None, ('fsdp', 'seq'))
The draws below stay inside these ranges and needn't reach their ends.
Inputs may be any that keep to these rules, and one draw needn't show every extreme that they name: `cond_pick`: each latent's row of cond_table.
All inputs are finite; a program needn't handle non-finite values.
Results may differ from the reference program's by a relative error of at most 0.023.
Values may be sent and summed in bfloat16 or wider, within the bound.
A program may use at most 320 MiB of HBM per device.

```python
import math
import jax
import jax.numpy as jnp
from jax import lax

D = 768
HEADS = 12
HEAD_DIM = 64
FF = 3072
COND_ROWS = 1000
LAYERS = 2
LATENTS = 32
LENGTH = 128


def touch_ends(result, key, least, high):
    dims = result.shape
    index_at = [jax.random.randint(jax.random.fold_in(key, axis), (), 0, dims[axis]) for axis in range(len(dims))]
    result = result.at[tuple(index_at)].set(least)
    longest = dims.index(max(dims))
    index_at[longest] = (index_at[longest] + 1) % dims[longest]
    return result.at[tuple(index_at)].set(high)


def block_scale(own_key, extent, cuts, low, high):
    gain, own = 1.0, jax.random.fold_in(own_key, 6)
    for position, parts in cuts:
        draws = jnp.exp(jax.random.uniform(jax.random.fold_in(own, position), (parts,), jnp.float32, low / len(cuts), high / len(cuts)))
        gain = gain * jnp.repeat(draws, extent[position] // parts).reshape([-1 if axis == position else 1 for axis in range(len(extent))])
    return gain


def normal_values(key, extent, spread, most, cuts=(), dtype=jnp.bfloat16):
    array = spread * jax.random.normal(key, extent, jnp.float32)
    if cuts:
        array = array * block_scale(key, extent, cuts, -0.22, 0.18)
    return jnp.clip(array, -most, most).astype(dtype)


def setup_inputs(seed: int = 0) -> dict:
    seeds = jax.random.split(jax.random.key(seed), 11)
    return {
        "latents": normal_values(seeds[0], (LATENTS, LENGTH, D), 1.0, 6.0, ((0, 16), (1, 2)), jnp.float32),
        "cond_pick": touch_ends(jax.random.randint(seeds[1], (LATENTS,), 0, COND_ROWS), jax.random.fold_in(seeds[1], 1), 0, COND_ROWS - 1).astype(jnp.int32),
        "cond_table": normal_values(seeds[2], (COND_ROWS, D), 1.0, 6.0, (), jnp.float32),
        "w_ada": normal_values(seeds[3], (LAYERS, D, 6 * D), D ** -0.5, 0.21875, ((2, 32),)),
        "b_ada": normal_values(seeds[4], (LAYERS, 6 * D), 0.5, 3.0, ((1, 32),)),
        "w_qkv": normal_values(seeds[5], (LAYERS, D, 3 * D), D ** -0.5, 0.21875, ((2, 32),)),
        "w_out": normal_values(seeds[6], (LAYERS, D, D), (max(1, 3 * D // LENGTH)) ** -0.5, 1.5, ((2, 32),)),
        "w_up": normal_values(seeds[7], (LAYERS, D, FF), D ** -0.5, 0.21875, ((2, 32),)),
        "w_down": normal_values(seeds[8], (LAYERS, FF, D), FF ** -0.5, 0.109375, ((1, 32),)),
        "cotangent": normal_values(seeds[9], (LATENTS, LENGTH, D), 1.0, 6.0, ((0, 16), (1, 2)), jnp.float32),
    }


HIGH = lax.Precision.HIGHEST
EPS = 1e-06

@jax.custom_vjp
def low(v):
    return lax.optimization_barrier(v.astype(jnp.bfloat16)).astype(jnp.float32)

@jax.custom_vjp
def low_back(v):
    return v

def low_keep(v):
    return (low(v), None)

def low_pass(kept, grad):
    return (grad,)

def back_keep(v):
    return (v, None)

def back_low(kept, grad):
    return (low(grad),)
low.defvjp(low_keep, low_pass)
low_back.defvjp(back_keep, back_low)

def layer_norm(values):
    centred = values - lax.optimization_barrier(jnp.mean(values, -1, keepdims=True))
    return centred * lax.rsqrt(lax.optimization_barrier(jnp.mean(centred * centred, -1, keepdims=True)) + EPS)

def gelu_tanh(values):
    return jax.nn.gelu(values, approximate=True)

def block(stream, silu_cond, w_ada, b_ada, w_qkv, w_out, w_up, w_down):
    group_size, length, model_width = stream.shape
    modulation = jnp.dot(silu_cond, w_ada, precision=HIGH) + b_ada
    pieces = [modulation[:, None, piece_index * model_width:(piece_index + 1) * model_width] for piece_index in range(6)]
    hidden_in = low(layer_norm(stream) * (1.0 + pieces[1]) + pieces[0])
    qkv_rows = jnp.einsum('gtd,de->gte', hidden_in, w_qkv, precision=HIGH)
    queries = low(low_back(qkv_rows[..., :model_width])).reshape(group_size, length, HEADS, HEAD_DIM)
    key_rows = low(low_back(qkv_rows[..., model_width:2 * model_width])).reshape(group_size, length, HEADS, HEAD_DIM)
    value_rows = low(low_back(qkv_rows[..., 2 * model_width:])).reshape(group_size, length, HEADS, HEAD_DIM)
    scores = low_back(jnp.einsum('gqhd,gkhd->ghqk', queries, key_rows, precision=HIGH) * HEAD_DIM ** (-0.5))
    soft_probs = low(jax.nn.softmax(scores, axis=-1))
    attn_mixed = jnp.einsum('ghqk,gkhd->gqhd', soft_probs, value_rows, precision=HIGH)
    attn_mixed = low(low_back(attn_mixed.reshape(group_size, length, model_width)))
    branch = low_back(jnp.einsum('gtd,de->gte', attn_mixed, w_out, precision=HIGH))
    middle = stream + pieces[2] * branch
    hidden_mlp = low(layer_norm(middle) * (1.0 + pieces[4]) + pieces[3])
    mlp_upper = low_back(jnp.einsum('gtd,df->gtf', hidden_mlp, w_up, precision=HIGH))
    active = low(gelu_tanh(mlp_upper))
    mlp_down = low_back(jnp.einsum('gtf,fd->gtd', active, w_down, precision=HIGH))
    return middle + pieces[5] * mlp_down

def forward_all(latents, cond_table, w_ada, b_ada, w_qkv, w_out, w_up, w_down, cond_pick):
    silu_cond = jax.nn.silu(cond_table[cond_pick])
    group_size = math.gcd(LATENTS, max(1, 4096 // LENGTH))
    step_count = LATENTS // group_size
    streams = latents.reshape(step_count, group_size, LENGTH, D)
    conditions = silu_cond.reshape(step_count, group_size, D)

    def advance(carry, item):
        stream, condition = item
        for layer_index in range(LAYERS):
            stream = block(stream, condition, w_ada[layer_index], b_ada[layer_index], w_qkv[layer_index], w_out[layer_index], w_up[layer_index], w_down[layer_index])
        return (carry, stream)
    _, results = lax.scan(jax.checkpoint(advance), jnp.zeros((), jnp.float32), (streams, conditions))
    return results.reshape(LATENTS, LENGTH, D)

def reference(latents, cond_pick, cond_table, w_ada, b_ada, w_qkv, w_out, w_up, w_down, cotangent):
    floats = [weight_arr.astype(jnp.float32) for weight_arr in (w_ada, b_ada, w_qkv, w_out, w_up, w_down)]

    def wrapped(latents_in, table_in, ada_in, bias_in, qkv_in, out_in, up_in, down_in):
        return forward_all(latents_in, table_in, ada_in, bias_in, qkv_in, out_in, up_in, down_in, cond_pick)
    output, pullback = jax.vjp(wrapped, latents, cond_table, floats[0], floats[1], floats[2], floats[3], floats[4], floats[5])
    grads = pullback(cotangent)
    return (output, grads[0], grads[1], grads[2], grads[3], grads[4], grads[5], grads[6], grads[7])
```

```python
import functools

import jax
import jax.numpy as jnp
from jax import lax
from jax.experimental import pallas as pl
from jax.experimental.pallas import tpu as pltpu
from jax.sharding import PartitionSpec as P

HEADS = 12
EPS = 1e-06
HIGH = lax.Precision.HIGHEST
BOTH = ("fsdp", "seq")
MESH = pl.DeviceIdType.MESH


def exchange_kernel(fsdp_size, seq_size, x_ref, y_ref, send_sem, recv_sem, local_sem):
    count = fsdp_size * seq_size
    me = lax.axis_index("fsdp") * seq_size + lax.axis_index("seq")

    def where(peer):
        return (peer // seq_size, peer % seq_size)

    barrier = pltpu.get_barrier_semaphore()

    def greet(step, carry):
        pl.semaphore_signal(
            barrier, inc=1, device_id=where((me + step) % count), device_id_type=MESH
        )
        return carry

    lax.fori_loop(1, count, greet, 0)
    own = pltpu.make_async_copy(x_ref.at[me], y_ref.at[me], local_sem)
    own.start()
    pl.semaphore_wait(barrier, count - 1)

    def copy_to(peer, source):
        return pltpu.make_async_remote_copy(
            src_ref=x_ref.at[peer],
            dst_ref=y_ref.at[source],
            send_sem=send_sem.at[peer],
            recv_sem=recv_sem.at[source],
            device_id=where(peer),
            device_id_type=MESH,
        )

    def send(step, carry):
        copy_to((me + step) % count, me).start()
        return carry

    def finish(step, carry):
        peer = (me + step) % count
        copy_to(peer, peer).wait()
        return carry

    lax.fori_loop(1, count, send, 0)
    own.wait()
    lax.fori_loop(1, count, finish, 0)


def exchange(blocks, sizes, call_id):
    fsdp_size, seq_size = sizes
    count = fsdp_size * seq_size
    vmem = pl.BlockSpec(memory_space=pltpu.VMEM)
    return pl.pallas_call(
        functools.partial(exchange_kernel, fsdp_size, seq_size),
        out_shape=jax.ShapeDtypeStruct(blocks.shape, blocks.dtype),
        in_specs=[vmem],
        out_specs=vmem,
        scratch_shapes=[
            pltpu.SemaphoreType.DMA((count,)),
            pltpu.SemaphoreType.DMA((count,)),
            pltpu.SemaphoreType.DMA,
        ],
        compiler_params=pltpu.CompilerParams(
            collective_id=call_id, has_side_effects=True, vmem_limit_bytes=40 * 1024 * 1024
        ),
    )(blocks)


def norm_rows(values):
    centred = values - jnp.mean(values, -1, keepdims=True)
    inverse = lax.rsqrt(jnp.mean(centred * centred, -1, keepdims=True) + EPS)
    return (centred * inverse, inverse)


def norm_back(normed, inverse, grad_in):
    return inverse * (
        grad_in
        - jnp.mean(grad_in, -1, keepdims=True)
        - normed * jnp.mean(grad_in * normed, -1, keepdims=True)
    )


def gelu_tanh(values):
    return jax.nn.gelu(values, approximate=True)


def mm(spec, left, right):
    return jnp.einsum(spec, left, right, preferred_element_type=jnp.float32)


def split_heads(rows):
    return rows.reshape(rows.shape[0], rows.shape[1], HEADS, rows.shape[2] // HEADS)


def gather_tokens(rows, whole):
    return rows if whole else lax.all_gather(rows, "seq", axis=1, tiled=True)


def layer_forward(stream, pieces, weights, whole):
    w_qkv, w_out, w_up, w_down = weights
    width = stream.shape[-1]
    normed, inverse = norm_rows(stream)
    hidden_in = (normed * (1.0 + pieces[1]) + pieces[0]).astype(jnp.bfloat16)
    qkv = mm("btd,ed->bte", hidden_in, w_qkv).astype(jnp.bfloat16)
    query_heads = split_heads(qkv[..., :width])
    key_heads = split_heads(gather_tokens(qkv[..., width : 2 * width], whole))
    value_heads = split_heads(gather_tokens(qkv[..., 2 * width :], whole))
    scores = mm("bqhd,bkhd->bhqk", query_heads, key_heads) * (width // HEADS) ** (-0.5)
    exp_scores = jnp.exp(scores - jnp.max(scores, -1, keepdims=True))
    soft_full = exp_scores / jnp.sum(exp_scores, -1, keepdims=True)
    soft_probs = soft_full.astype(jnp.bfloat16)
    mixed = mm("bhqk,bkhd->bqhd", soft_probs, value_heads).reshape(stream.shape)
    mixed = mixed.astype(jnp.bfloat16)
    branch = mm("btd,ed->bte", mixed, w_out)
    middle = stream + pieces[2] * branch
    normed_mlp, inverse_mlp = norm_rows(middle)
    hidden_mlp = (normed_mlp * (1.0 + pieces[4]) + pieces[3]).astype(jnp.bfloat16)
    upper = mm("btd,fd->btf", hidden_mlp, w_up)
    active = gelu_tanh(upper).astype(jnp.bfloat16)
    down = mm("btf,fd->btd", active, w_down)
    saved = (
        normed,
        inverse,
        hidden_in,
        query_heads,
        key_heads,
        value_heads,
        soft_full,
        mixed,
        branch,
        normed_mlp,
        inverse_mlp,
        hidden_mlp,
        upper,
        active,
        down,
    )
    return (middle + pieces[5] * down, saved)


def layer_backward(saved, pieces, weights, grad_out, whole):
    w_qkv, w_out, w_up, w_down = weights
    (
        normed,
        inverse,
        hidden_in,
        query_heads,
        key_heads,
        value_heads,
        soft_full,
        mixed,
        branch,
        normed_mlp,
        inverse_mlp,
        hidden_mlp,
        upper,
        active,
        down,
    ) = saved
    width = grad_out.shape[-1]
    scale_factor = (width // HEADS) ** (-0.5)
    grad_gate_mlp = jnp.sum(grad_out * down, 1)
    grad_down = (pieces[5] * grad_out).astype(jnp.bfloat16)
    weight_down = mm("btf,btd->fd", active, grad_down).astype(jnp.bfloat16)
    grad_active = mm("btd,fd->btf", grad_down, w_down)
    _, gelu_pull = jax.vjp(gelu_tanh, upper)
    grad_upper = gelu_pull(grad_active)[0].astype(jnp.bfloat16)
    weight_up = mm("btf,btd->fd", grad_upper, hidden_mlp).astype(jnp.bfloat16)
    grad_hidden_mlp = mm("btf,fd->btd", grad_upper, w_up)
    grad_shift_mlp = jnp.sum(grad_hidden_mlp, 1)
    grad_scale_mlp = jnp.sum(grad_hidden_mlp * normed_mlp, 1)
    grad_middle = grad_out + norm_back(normed_mlp, inverse_mlp, grad_hidden_mlp * (1.0 + pieces[4]))
    grad_gate_attn = jnp.sum(grad_middle * branch, 1)
    grad_branch = (pieces[2] * grad_middle).astype(jnp.bfloat16)
    weight_out = mm("bte,btd->ed", grad_branch, mixed).astype(jnp.bfloat16)
    grad_mixed = split_heads(mm("bte,ed->btd", grad_branch, w_out).astype(jnp.bfloat16))
    soft_probs = soft_full.astype(jnp.bfloat16)
    grad_probs = mm("bqhd,bkhd->bhqk", grad_mixed, value_heads)
    grad_values = mm("bhqk,bqhd->bkhd", soft_probs, grad_mixed)
    inner = jnp.sum(grad_probs * soft_full, -1, keepdims=True)
    grad_scores = (soft_full * (grad_probs - inner)).astype(jnp.bfloat16)
    grad_queries = mm("bhqk,bkhd->bqhd", grad_scores, key_heads) * scale_factor
    grad_keys = mm("bhqk,bqhd->bkhd", grad_scores, query_heads) * scale_factor
    rows = grad_out.shape[:2]
    grad_queries = grad_queries.reshape(grad_out.shape).astype(jnp.bfloat16)
    grad_keys = grad_keys.reshape(rows[0], -1, width).astype(jnp.bfloat16)
    grad_values = grad_values.reshape(rows[0], -1, width).astype(jnp.bfloat16)
    if not whole:
        grad_keys = lax.psum_scatter(grad_keys, "seq", scatter_dimension=1, tiled=True)
        grad_values = lax.psum_scatter(grad_values, "seq", scatter_dimension=1, tiled=True)
    grad_qkv = jnp.concatenate([grad_queries, grad_keys, grad_values], -1)
    weight_qkv = mm("bte,btd->ed", grad_qkv, hidden_in).astype(jnp.bfloat16)
    grad_hidden = mm("bte,ed->btd", grad_qkv, w_qkv)
    grad_shift_attn = jnp.sum(grad_hidden, 1)
    grad_scale_attn = jnp.sum(grad_hidden * normed, 1)
    grad_stream = grad_middle + norm_back(normed, inverse, grad_hidden * (1.0 + pieces[1]))
    grad_mod = jnp.concatenate(
        [
            grad_shift_attn,
            grad_scale_attn,
            grad_gate_attn,
            grad_shift_mlp,
            grad_scale_mlp,
            grad_gate_mlp,
        ],
        -1,
    )
    return (grad_stream, (weight_qkv, weight_out, weight_up, weight_down), grad_mod)


def swap_tokens(values, seq_size):
    me = lax.axis_index("seq")
    keep = lax.dynamic_index_in_dim(values, me, 0, keepdims=False)
    give = lax.dynamic_index_in_dim(values, 1 - me, 0, keepdims=False)
    other = lax.ppermute(give, "seq", [(0, 1), (1, 0)])
    return jnp.concatenate([keep, other], 0)[None]


def swap_back(values, seq_size):
    me = lax.axis_index("seq")
    tokens = values.shape[1] // 2
    keep, give = values[0, :tokens], values[0, tokens:]
    other = lax.ppermute(give, "seq", [(0, 1), (1, 0)])
    first = jnp.where(me == 0, keep, other)
    second = jnp.where(me == 0, other, keep)
    return jnp.stack([first, second])


def local(sizes, latents, cond_pick, cond_table, w_ada, b_ada, w_qkv, w_out, w_up, w_down, cotangent):
    fsdp_size, seq_size = sizes
    count = fsdp_size * seq_size
    layers, width, ada_cols = w_ada.shape
    local_latents = latents.shape[0]
    all_latents = local_latents * fsdp_size
    whole = seq_size == 2 and local_latents == 2
    fsdp_me = lax.axis_index("fsdp")
    seq_me = lax.axis_index("seq")

    parts = [w_qkv.shape[2], w_out.shape[2], w_up.shape[2], w_down.shape[1]]
    starts = [sum(parts[:index]) for index in range(5)]
    gathered = []
    for layer in range(layers):
        packed = jnp.concatenate(
            [w_qkv[layer].T, w_out[layer].T, w_up[layer].T, w_down[layer]], 0
        )
        gathered.append(lax.all_gather(packed, BOTH, axis=0, tiled=False))

    def unpack(block):
        return tuple(
            block[:, starts[index] : starts[index + 1]].reshape(-1, width) for index in range(4)
        )

    pick_rows = jnp.broadcast_to(
        jnp.pad(cond_pick.astype(jnp.float32), (0, 128 - local_latents))[None, None],
        (count, 8, 128),
    )
    picks = exchange(pick_rows, sizes, 0)[::seq_size, 0, :local_latents].reshape(-1)
    picks = picks.astype(jnp.int32)
    table_rows = cond_table.shape[0]
    one_hot = (picks[:, None] == jnp.arange(table_rows, dtype=jnp.int32)[None, :]).astype(
        jnp.float32
    )
    condition_all = jnp.dot(one_hot, cond_table, precision=HIGH, preferred_element_type=jnp.float32)
    silu_all = jax.nn.silu(condition_all)
    mod_cols = jnp.stack(
        [
            jnp.dot(
                silu_all,
                w_ada[layer].astype(jnp.float32),
                precision=HIGH,
                preferred_element_type=jnp.float32,
            )
            + b_ada[layer].astype(jnp.float32)
            for layer in range(layers)
        ]
    )
    mod_send = mod_cols.reshape(layers, fsdp_size, 1, local_latents, ada_cols)
    mod_send = jnp.broadcast_to(
        mod_send.transpose(1, 2, 0, 3, 4),
        (fsdp_size, seq_size, layers, local_latents, ada_cols),
    ).reshape(count, layers * local_latents, ada_cols)
    mod_mine = (
        exchange(mod_send, sizes, 1)
        .reshape(count, layers, local_latents, ada_cols)
        .transpose(1, 2, 0, 3)
        .reshape(layers, local_latents, 6, width)
    )
    if whole:
        mod_mine = lax.dynamic_slice_in_dim(mod_mine, seq_me, 1, 1)

    stream = swap_tokens(latents, seq_size) if whole else latents
    grad_stream = swap_tokens(cotangent, seq_size) if whole else cotangent
    weights_of, pieces_of, saved_of = [], [], []
    for layer in range(layers):
        weights_of.append(unpack(gathered[layer]))
        pieces_of.append([mod_mine[layer, :, None, piece] for piece in range(6)])
        stream, saved = layer_forward(stream, pieces_of[layer], weights_of[layer], whole)
        saved_of.append(saved)
    output = swap_back(stream, seq_size) if whole else stream

    summed = [None] * layers
    mod_grads = [None] * layers
    for layer in reversed(range(layers)):
        grad_stream, grads, mod_grads[layer] = layer_backward(
            saved_of[layer], pieces_of[layer], weights_of[layer], grad_stream, whole
        )
        packed = jnp.concatenate([grad.reshape(count, -1, width) for grad in grads], 1)
        summed[layer] = lax.psum_scatter(packed, BOTH, scatter_dimension=0, tiled=False)
    grad_latents = swap_back(grad_stream, seq_size) if whole else grad_stream

    grad_mod = jnp.stack(mod_grads)
    rows = grad_mod.shape[1]
    mod_send = (
        grad_mod.reshape(layers, rows, count, ada_cols)
        .transpose(2, 0, 1, 3)
        .reshape(count, layers * rows, ada_cols)
    )
    mod_all = exchange(mod_send, sizes, 2).reshape(fsdp_size, seq_size, layers, rows, ada_cols)
    if whole:
        mod_all = mod_all.transpose(2, 0, 1, 3, 4)
    else:
        mod_all = jnp.sum(mod_all, 1).transpose(1, 0, 2, 3)
    mod_all = mod_all.reshape(layers, all_latents, ada_cols)
    grad_w_ada = jnp.stack(
        [
            jnp.dot(
                silu_all.T, mod_all[layer], precision=HIGH, preferred_element_type=jnp.float32
            )
            for layer in range(layers)
        ]
    )
    grad_b_ada = jnp.sum(mod_all, 1)
    grad_cond = sum(
        jnp.einsum(
            "be,de->bd",
            mod_all[layer],
            w_ada[layer].astype(jnp.float32),
            precision=HIGH,
            preferred_element_type=jnp.float32,
        )
        for layer in range(layers)
    )
    table_cols = width // count
    cond_send = grad_cond.reshape(all_latents, count, table_cols).transpose(1, 0, 2)
    grad_cond_cols = jnp.sum(exchange(cond_send, sizes, 3), 0)
    me = fsdp_me * seq_size + seq_me
    cond_cols = lax.dynamic_slice_in_dim(condition_all, me * table_cols, table_cols, 1)
    _, silu_pull = jax.vjp(jax.nn.silu, cond_cols)
    grad_table = jnp.dot(
        one_hot.T,
        silu_pull(grad_cond_cols)[0],
        precision=HIGH,
        preferred_element_type=jnp.float32,
    )

    stacked = jnp.stack(summed).astype(jnp.float32)
    grads = [stacked[:, starts[index] : starts[index + 1]] for index in range(4)]
    return (
        output,
        grad_latents,
        grad_table,
        grad_w_ada,
        grad_b_ada,
        jnp.swapaxes(grads[0], 1, 2),
        jnp.swapaxes(grads[1], 1, 2),
        jnp.swapaxes(grads[2], 1, 2),
        grads[3],
    )


def solution(mesh):
    sizes = (mesh.shape["fsdp"], mesh.shape["seq"])
    columns = P(None, None, BOTH)
    tokens = P("fsdp", "seq", None)
    return jax.shard_map(
        functools.partial(local, sizes),
        mesh=mesh,
        in_specs=(
            tokens,
            P("fsdp"),
            P(),
            columns,
            P(None, BOTH),
            columns,
            columns,
            columns,
            P(None, BOTH, None),
            tokens,
        ),
        out_specs=(
            tokens,
            tokens,
            P(None, BOTH),
            columns,
            P(None, BOTH),
            columns,
            columns,
            columns,
            P(None, BOTH, None),
        ),
        check_vma=False,
    )
```
